32 devices in a mesh: expert: 8 (over z, y), tensor: 4 (over x, core).
Axes of the slice: x: 2, y: 2, z: 4, core: 2. Of those that a mesh axis runs over, the one named last changes fastest.
Arguments:
- tokens: bfloat16 [4096, 2048], P('expert'), may hold values from -6 to 6
- segments: int32 [8, 512], P('expert'), may hold values from 0 to 2, never falling along the last dimension, each value on 1 to 256 neighbouring positions
- routes: int32 [4096, 6], P('expert'), may hold values from 0 to 15, all different within a row; in each aligned block of 512 rows (0 to 511, 512 to 1023, ...) at most 320 rows name the same one
- cotangent: bfloat16 [4096, 2048], P('expert'), may hold values from -6 to 6
- norm_in: bfloat16 [2048], P('expert'), may hold values from 0.5 to 1.5
- w_query: bfloat16 [2048, 3072], P('expert', 'tensor'), may hold values from -0.125 to 0.125
- w_latent: bfloat16 [2048, 576], P('expert'), may hold values from -0.125 to 0.125
- norm_latent: bfloat16 [512], P('expert'), may hold values from 0.5 to 1.5
- w_keyval: bfloat16 [512, 4096], P('expert', 'tensor'), may hold values from -0.25 to 0.25
- w_out: bfloat16 [2048, 2048], P('expert', 'tensor'), may hold values from -0.5 to 0.5
- norm_mid: bfloat16 [2048], P('expert'), may hold values from 0.5 to 1.5
- w_router: bfloat16 [2048, 16], P('expert'), may hold values from -0.0625 to 0.0625
- shared_gate: bfloat16 [2048, 2816], P('expert', 'tensor'), may hold values from -0.125 to 0.125
- shared_up: bfloat16 [2048, 2816], P('expert', 'tensor'), may hold values from -0.125 to 0.125
- shared_down: bfloat16 [2048, 2816], P('expert', 'tensor'), may hold values from -0.109375 to 0.109375
- expert_gate: bfloat16 [16, 2048, 1408], P('expert', None, 'tensor'), may hold values from -0.125 to 0.125
- expert_up: bfloat16 [16, 2048, 1408], P('expert', None, 'tensor'), may hold values from -0.125 to 0.125
- expert_down: bfloat16 [16, 1408, 2048], P('expert', 'tensor'), may hold values from -0.15625 to 0.15625
Outputs:
- mixed: bfloat16 [4096, 2048], P('expert', 'tensor')
- tokens_grad: bfloat16 [4096, 2048], P(('expert', 'tensor'))
- grad_norm_in: float32 [2048], P(('expert', 'tensor'))
- grad_w_query: float32 [2048, 3072], P('expert', 'tensor')
- grad_w_latent: float32 [2048, 576], P(('expert', 'tensor'))
- grad_norm_latent: float32 [512], P(('expert', 'tensor'))
- grad_w_keyval: float32 [512, 4096], P('expert', 'tensor')
- grad_w_out: float32 [2048, 2048], P('expert', 'tensor')
- grad_norm_mid: float32 [2048], P(('expert', 'tensor'))
- grad_w_router: float32 [2048, 16], P(('expert', 'tensor'))
- grad_shared_gate: float32 [2048, 2816], P('expert', 'tensor')
- grad_shared_up: float32 [2048, 2816], P('expert', 'tensor')
- grad_shared_down: float32 [2048, 2816], P('expert', 'tensor')
- grad_expert_gate: float32 [16, 2048, 1408], P('expert', None, 'tensor')
- grad_expert_up: float32 [16, 2048, 1408], P('expert', None, 'tensor')
- grad_expert_down: float32 [16, 1408, 2048], P('expert', 'tensor')
The draws below stay inside these ranges and needn't reach their ends.
Inputs may be any that keep to these rules, and one draw needn't show every extreme that they name: `segments`: each row is one sequence of 512 tokens; document numbers never fall along it, each document has 1 to 256 tokens and one has exactly 256. `routes`: A token's 6 experts differ. In each aligned block of 512 rows (one sequence) no expert is named by more than 320 rows, a bound that some block reaches.
All inputs are finite; a program needn't handle non-finite values.
Results may differ from the reference program's by a relative error of at most 0.025.
Values may be sent and summed in bfloat16 or wider, within the bound.
A program may use at most 384 MiB of HBM per device.

```python
import math
import jax
import jax.numpy as jnp
import numpy as np
from jax import lax

D = 2048
HEADS = 16
NOPE = 128
ROPE = 64
VD = 128
KVR = 512
EFF = 1408
SHARED = 2816
TOP = 6
TOK_DEV = 512
DOCS = 3
EXPERTS = 16
TOKENS = 4096
NSEQ = 8
CAP = 320
DOC_MOST = 256
N_TENSOR = 4


def steps_of(stream_key, dims, pieces, least, high):
    factor_of, own = 1.0, jax.random.fold_in(stream_key, 6)
    for position, blocks in pieces:
        draws = jnp.exp(jax.random.uniform(jax.random.fold_in(own, position), (blocks,), jnp.float32, least / len(pieces), high / len(pieces)))
        factor_of = factor_of * jnp.repeat(draws, dims[position] // blocks).reshape([-1 if axis == position else 1 for axis in range(len(dims))])
    return factor_of


def split_up(count, total, limit, slope):
    weights = [(1 << 20) // math.isqrt(standing ** slope) + 1 for standing in range(2, count + 1)]
    rest, holding = total - limit - (count - 1), [1] * (count - 1)
    while rest > 0:
        candidates = [i for i in range(count - 1) if holding[i] < limit]
        mass, remaining = sum([weights[i] for i in candidates]), rest
        for i in candidates:
            more = min(limit - holding[i], max(1, remaining * weights[i] // mass), rest)
            holding[i] = holding[i] + more
            rest = rest - more
    return np.array([limit] + holding)


def ragged_sizes(own_key, amount, total, limit, slope):
    if amount == 2:
        one = jax.random.randint(own_key, (), max(1, total - limit), min(limit, total - 1) + 1)
        return jnp.stack([one, total - one])
    tallies = jnp.asarray(split_up(amount, total, limit, slope), jnp.int32)
    pairs = (amount - 1) // 2
    donor, taker = tallies[1:1 + 2 * pairs:2], tallies[2:2 + 2 * pairs:2]
    slack = jnp.minimum(donor - 1, limit - taker)
    moved = jax.random.randint(jax.random.fold_in(own_key, 1), (pairs,), 0, 1 << 20) % (slack + 1)
    tallies = tallies.at[1:1 + 2 * pairs:2].set(donor - moved).at[2:2 + 2 * pairs:2].set(taker + moved)
    return tallies[jax.random.permutation(jax.random.fold_in(own_key, 2), amount)]


def deal_out(stream_key, own, number, rows, count, top, limit, skew):
    sequence = jax.random.permutation(stream_key, count)
    crowded, usual = shares(count, rows * top, limit, skew, True), shares(count, rows * top, limit, skew, False)
    places = jnp.arange(count)

    def named(lengths, offset_by):
        used = int((lengths > 0).sum())
        fixed = max(1, used // 4)
        moved = fixed + (places - fixed + offset_by * (used - fixed)) % max(1, count - fixed)
        return jnp.zeros((count,), jnp.int32).at[sequence[jnp.where(places < fixed, places, moved)]].set(jnp.asarray(lengths, jnp.int32))

    lengths = jnp.where(number % 4 == 0, named(crowded, number // 4), named(usual, number - number // 4 - 1))
    mixed = jax.random.permutation(jax.random.fold_in(own, 3), count)
    source_of, sink = mixed[0:count // 2 * 2:2], mixed[1:count // 2 * 2:2]
    margin = jnp.minimum(lengths[source_of] - 1, limit - lengths[sink]) // 2
    margin = jnp.where((source_of == sequence[0]) | (sink == sequence[0]) | (lengths[sink] == 0), 0, jnp.maximum(margin, 0))
    moved = jax.random.randint(jax.random.fold_in(own, 4), (count // 2,), 0, 1 << 20) % (margin + 1)
    lengths = lengths.at[source_of].add(-moved).at[sink].add(moved)
    items = jnp.searchsorted(jnp.cumsum(lengths), jnp.arange(rows * top), side="right").astype(jnp.int32)
    listing = items.reshape(top, rows).T
    listing = listing[jax.random.permutation(jax.random.fold_in(own, 1), rows)]
    offset_by = jax.random.randint(jax.random.fold_in(own, 2), (rows, 1), 0, top)
    return jnp.take_along_axis(listing, (jnp.arange(top)[None, :] + offset_by) % top, axis=1)


def shares(number_of, total, bound, lean, full):
    weights = [(1 << 20) // math.isqrt(grade ** lean) + 1 for grade in range(1, number_of + 1)]
    largest = bound if full else min(bound, max(-(-total // number_of), total * weights[0] // sum(weights)))
    least = 1 if total - largest >= number_of - 1 else 0
    counts, spare = [largest] + [least] * (number_of - 1), total - largest - least * (number_of - 1)
    while spare > 0:
        candidates = [i for i in range(1, number_of) if counts[i] < largest] or [i for i in range(1, number_of) if counts[i] < bound]
        whole, remaining = sum([weights[i] for i in candidates]), spare
        for i in candidates:
            extra = min(bound - counts[i], max(1, remaining * weights[i] // whole), spare)
            counts[i] = counts[i] + extra
            spare = spare - extra
    return np.array(counts)


def bell_draw(own_key, dims, width, most, shards=(), held_as=jnp.bfloat16):
    values = width * jax.random.normal(own_key, dims, jnp.float32)
    if shards:
        values = values * steps_of(own_key, dims, shards, -0.22, 0.18)
    return jnp.clip(values, -most, most).astype(held_as)


def setup_inputs(seed: int = 0) -> dict:
    splits = jax.random.split(jax.random.key(seed), 19)
    tokens = bell_draw(splits[0], (TOKENS, D), 1.0, 6.0, ((0, 8),))
    segments = jax.vmap(lambda own: jnp.searchsorted(jnp.cumsum(ragged_sizes(own, DOCS, TOK_DEV, DOC_MOST, 1)), jnp.arange(TOK_DEV), side="right"))(jax.random.split(splits[1], NSEQ)).reshape((NSEQ, TOK_DEV)).astype(jnp.int32)
    routes_keys = jax.random.split(jax.random.fold_in(splits[2], 1), TOKENS // TOK_DEV)
    routes_turns = jax.random.permutation(jax.random.fold_in(splits[2], 3), TOKENS // TOK_DEV)
    routes = jax.vmap(lambda own, number: deal_out(jax.random.fold_in(splits[2], 2), own, number, TOK_DEV, EXPERTS, TOP, CAP, 1))(routes_keys, routes_turns).reshape((TOKENS, TOP))
    cotangent = bell_draw(splits[3], (TOKENS, D), 1.0, 6.0, ((0, 8),))
    norm_in = jnp.clip(1.0 + 0.1 * jax.random.normal(splits[4], (D,), jnp.float32), 0.5, 1.5).astype(jnp.bfloat16)
    w_query = bell_draw(splits[5], (D, HEADS * (NOPE + ROPE)), D ** -0.5, 0.125, ((0, 8), (1, 4)))
    w_latent = bell_draw(splits[6], (D, KVR + ROPE), D ** -0.5, 0.125, ((0, 8),))
    norm_latent = jnp.clip(1.0 + 0.1 * jax.random.normal(splits[7], (KVR,), jnp.float32), 0.5, 1.5).astype(jnp.bfloat16)
    w_keyval = bell_draw(splits[8], (KVR, HEADS * (NOPE + VD)), KVR ** -0.5, 0.25, ((0, 8), (1, 4)))
    w_out = bell_draw(splits[9], (D, HEADS * VD), (HEADS * VD // 16) ** -0.5, 0.5, ((0, 8), (1, 4)))
    norm_mid = jnp.clip(1.0 + 0.1 * jax.random.normal(splits[10], (D,), jnp.float32), 0.5, 1.5).astype(jnp.bfloat16)
    w_router = bell_draw(splits[11], (D, EXPERTS), (4 * D) ** -0.5, 0.0625, ((0, 8),))
    shared_gate = bell_draw(splits[12], (D, SHARED), D ** -0.5, 0.125, ((0, 8), (1, 4)))
    shared_up = bell_draw(splits[13], (D, SHARED), D ** -0.5, 0.125, ((0, 8), (1, 4)))
    shared_down = bell_draw(splits[14], (D, SHARED), SHARED ** -0.5, 0.109375, ((0, 8), (1, 4)))
    expert_gate = bell_draw(splits[15], (EXPERTS, D, EFF), D ** -0.5, 0.125, ((0, 8), (2, 4)))
    expert_up = bell_draw(splits[16], (EXPERTS, D, EFF), D ** -0.5, 0.125, ((0, 8), (2, 4)))
    expert_down = bell_draw(splits[17], (EXPERTS, EFF, D), EFF ** -0.5, 0.15625, ((0, 8), (1, 4)))
    return dict(tokens=tokens, segments=segments, routes=routes, cotangent=cotangent, norm_in=norm_in, w_query=w_query, w_latent=w_latent, norm_latent=norm_latent, w_keyval=w_keyval, w_out=w_out, norm_mid=norm_mid, w_router=w_router, shared_gate=shared_gate, shared_up=shared_up, shared_down=shared_down, expert_gate=expert_gate, expert_up=expert_up, expert_down=expert_down)


@jax.custom_vjp
def low(v):
    return lax.optimization_barrier(v.astype(jnp.bfloat16)).astype(jnp.float32)

@jax.custom_vjp
def low_back(v):
    return v

def low_keep(v):
    return (low(v), None)

def low_pass(kept, grad):
    return (grad,)

def back_keep(v):
    return (v, None)

def back_low(kept, grad):
    return (low(grad),)
low.defvjp(low_keep, low_pass)
low_back.defvjp(back_keep, back_low)
EPS = 1e-06
ROUTE_SCALE = 2.446
THETA = 50000.0
NEG = -1e+30
HIGH = lax.Precision.HIGHEST

def inv_rms(vec_in):
    return lax.rsqrt(lax.optimization_barrier(jnp.mean(vec_in * vec_in, axis=-1, keepdims=True)) + EPS)

def doc_positions(seg_ids):
    row_index = jnp.arange(seg_ids.shape[0], dtype=jnp.int32)
    starts = jnp.concatenate([jnp.ones((1,), jnp.int32), (seg_ids[1:] != seg_ids[:-1]).astype(jnp.int32)])
    first_idx = lax.cummax(jnp.where(starts > 0, row_index, jnp.zeros_like(row_index)), axis=0)
    return row_index - first_idx

def rope_tables(positions):
    half_dim = ROPE // 2
    freqs = THETA ** (-(jnp.arange(half_dim, dtype=jnp.float32) * 2.0 / ROPE))
    angles = positions.astype(jnp.float32)[:, None] * freqs[None, :]
    return (jnp.cos(angles), jnp.sin(angles))

def rotate(vec_in, cos_tab, sin_tab):
    half_dim = vec_in.shape[-1] // 2
    first_h = vec_in[..., :half_dim]
    second_h = vec_in[..., half_dim:]
    return jnp.concatenate([first_h * cos_tab - second_h * sin_tab, first_h * sin_tab + second_h * cos_tab], axis=-1)

def routed_part(normed_mid, route, gate_weights, expert_gate, expert_up, expert_down):
    seq_len = normed_mid.shape[0]
    flat_route = route.reshape(-1)
    onehot = (flat_route[:, None] == jnp.arange(EXPERTS, dtype=jnp.int32)[None, :]).astype(jnp.int32)
    slot_no = lax.optimization_barrier(jnp.sum(jnp.cumsum(onehot, axis=0) * onehot, axis=1)) - 1
    dest_idx = flat_route * CAP + slot_no
    source_tok = jnp.zeros((EXPERTS * CAP,), jnp.int32).at[dest_idx].set(jnp.arange(seq_len * TOP, dtype=jnp.int32) // TOP)
    live_mask = jnp.zeros((EXPERTS * CAP,), jnp.float32).at[dest_idx].set(1.0)
    slot_rows = (normed_mid[source_tok] * live_mask[:, None]).reshape(EXPERTS, CAP, D)
    block_units = EFF // N_TENSOR
    summed = jnp.zeros((EXPERTS, CAP, D), jnp.float32)
    for piece_no in range(N_TENSOR):
        lower = piece_no * block_units
        upper = lower + block_units
        my_rows = low_back(slot_rows)
        gate_x = low_back(jnp.einsum('ecd,edf->ecf', my_rows, expert_gate[:, :, lower:upper], precision=HIGH))
        up_x = low_back(jnp.einsum('ecd,edf->ecf', my_rows, expert_up[:, :, lower:upper], precision=HIGH))
        hidden_x = low(jax.nn.silu(gate_x) * up_x)
        summed = summed + low(jnp.einsum('ecf,efd->ecd', hidden_x, expert_down[:, lower:upper, :], precision=HIGH))
    outputs = low_back(summed).reshape(EXPERTS * CAP, D)
    picked = outputs[dest_idx].reshape(seq_len, TOP, D)
    return jnp.einsum('lk,lkd->ld', gate_weights, picked, precision=HIGH)

def sequence_forward(params, tok_rows, seg_ids, route):
    norm_in, w_query, w_latent, norm_latent, w_keyval, w_out, norm_mid, w_router, shared_gate, shared_up, shared_down, expert_gate, expert_up, expert_down = params
    seq_len = tok_rows.shape[0]
    normed = low(tok_rows * inv_rms(tok_rows) * norm_in)
    query_lin = low_back(jnp.dot(normed, w_query, precision=HIGH)).reshape(seq_len, HEADS, NOPE + ROPE)
    cos_tab, sin_tab = rope_tables(doc_positions(seg_ids))
    queries = low(jnp.concatenate([query_lin[..., :NOPE], rotate(query_lin[..., NOPE:], cos_tab[:, None, :], sin_tab[:, None, :])], axis=-1))
    latent_all = jnp.dot(normed, w_latent, precision=HIGH)
    latent = latent_all[:, :KVR]
    latent_n = low(latent * inv_rms(latent) * norm_latent)
    keyval = low_back(jnp.dot(latent_n, w_keyval, precision=HIGH)).reshape(seq_len, HEADS, NOPE + VD)
    key_rope = low(rotate(latent_all[:, KVR:], cos_tab, sin_tab))
    key_nope = low(keyval[..., :NOPE])
    values = low(keyval[..., NOPE:])
    scores = jnp.einsum('qhd,khd->hqk', queries[..., :NOPE], key_nope, precision=HIGH)
    scores = scores + jnp.einsum('qhd,kd->hqk', queries[..., NOPE:], key_rope, precision=HIGH)
    scores = low_back(scores * (NOPE + ROPE) ** (-0.5))
    row_index = jnp.arange(seq_len, dtype=jnp.int32)
    allowed = (seg_ids[:, None] == seg_ids[None, :]) & (row_index[:, None] >= row_index[None, :])
    scores = jnp.where(allowed[None], scores, NEG)
    softmaxed = jax.nn.softmax(scores, axis=-1)
    attended = low_back(low(jnp.einsum('hqk,khd->qhd', low(softmaxed), values, precision=HIGH))).reshape(seq_len, HEADS * VD)
    attn_out = low_back(jnp.dot(attended, w_out.T, precision=HIGH))
    residual = tok_rows + attn_out
    normed_mid = low(residual * inv_rms(residual) * norm_mid)
    router_prob = jax.nn.sigmoid(jnp.dot(normed_mid, w_router, precision=HIGH))
    chosen = jnp.take_along_axis(router_prob, route, axis=1)
    gate_weights = ROUTE_SCALE * chosen / lax.optimization_barrier(jnp.sum(chosen, axis=1, keepdims=True))
    gate_sh = low_back(jnp.dot(normed_mid, shared_gate, precision=HIGH))
    up_sh = low_back(jnp.dot(normed_mid, shared_up, precision=HIGH))
    hidden_sh = low(jax.nn.silu(gate_sh) * up_sh)
    shared_out = jnp.dot(hidden_sh, shared_down.T, precision=HIGH)
    routed = routed_part(normed_mid, route, gate_weights, expert_gate, expert_up, expert_down)
    return low(residual + shared_out + routed)

def reference(tokens, segments, routes, cotangent, norm_in, w_query, w_latent, norm_latent, w_keyval, w_out, norm_mid, w_router, shared_gate, shared_up, shared_down, expert_gate, expert_up, expert_down):
    params = tuple((weight.astype(jnp.float32) for weight in (norm_in, w_query, w_latent, norm_latent, w_keyval, w_out, norm_mid, w_router, shared_gate, shared_up, shared_down, expert_gate, expert_up, expert_down)))
    inputs = tokens.astype(jnp.float32).reshape(NSEQ, TOK_DEV, D)
    route_seq = routes.reshape(NSEQ, TOK_DEV, TOP)

    def forward(weights, tok_all):

        def per_seq(seq_item):
            return sequence_forward(weights, seq_item[0], seq_item[1], seq_item[2])
        return lax.map(jax.checkpoint(per_seq), (tok_all, segments, route_seq))
    mixed, pullback = jax.vjp(forward, params, inputs)
    weight_grads, tok_grad = pullback(cotangent.astype(jnp.float32).reshape(NSEQ, TOK_DEV, D))
    grad_norm_in, grad_w_query, grad_w_latent, grad_norm_latent, grad_w_keyval, grad_w_out, grad_norm_mid, grad_w_router, grad_shared_gate, grad_shared_up, grad_shared_down, grad_expert_gate, grad_expert_up, grad_expert_down = weight_grads
    return (mixed.reshape(TOKENS, D).astype(jnp.bfloat16), tok_grad.reshape(TOKENS, D).astype(jnp.bfloat16), grad_norm_in, grad_w_query, grad_w_latent, grad_norm_latent, grad_w_keyval, grad_w_out, grad_norm_mid, grad_w_router, grad_shared_gate, grad_shared_up, grad_shared_down, grad_expert_gate, grad_expert_up, grad_expert_down)
```

```python
import itertools
import math

import jax
import jax.numpy as jnp
from jax import lax
from jax.experimental import pallas as pl
from jax.experimental.pallas import tpu as pltpu
from jax.sharding import PartitionSpec as P

D = 2048
NOPE = 128
ROPE = 64
VD = 128
KVR = 512
TOP = 6


EPS = 1e-06
ROUTE_SCALE = 2.446
THETA = 50000.0
NEG = -1e30
HIGH = lax.Precision.HIGHEST


def inv_rms(vec_in):
    return lax.rsqrt(jnp.mean(vec_in * vec_in, axis=-1, keepdims=True) + EPS)


def doc_positions(seg_ids):
    row_index = jnp.arange(seg_ids.shape[0], dtype=jnp.int32)
    starts = jnp.concatenate(
        [jnp.ones((1,), jnp.int32), (seg_ids[1:] != seg_ids[:-1]).astype(jnp.int32)]
    )
    first_idx = lax.cummax(jnp.where(starts > 0, row_index, jnp.zeros_like(row_index)), axis=0)
    return row_index - first_idx


def rope_tables(positions):
    half_dim = ROPE // 2
    freqs = THETA ** (-(jnp.arange(half_dim, dtype=jnp.float32) * 2.0 / ROPE))
    angles = positions.astype(jnp.float32)[:, None] * freqs[None, :]
    return (jnp.cos(angles), jnp.sin(angles))


def rotate(vec_in, cos_tab, sin_tab):
    half_dim = vec_in.shape[-1] // 2
    first_h = vec_in[..., :half_dim]
    second_h = vec_in[..., half_dim:]
    return jnp.concatenate(
        [first_h * cos_tab - second_h * sin_tab, first_h * sin_tab + second_h * cos_tab], axis=-1
    )


def unrotate(grad_in, cos_tab, sin_tab):
    half_dim = grad_in.shape[-1] // 2
    first_g = grad_in[..., :half_dim]
    second_g = grad_in[..., half_dim:]
    return jnp.concatenate(
        [first_g * cos_tab + second_g * sin_tab, second_g * cos_tab - first_g * sin_tab], axis=-1
    )


def dot_plain(left_m, right_m):
    return jnp.dot(left_m, right_m, preferred_element_type=jnp.float32)


def dot_last(left_m, right_m):
    return lax.dot_general(
        left_m, right_m, (((1,), (1,)), ((), ())), preferred_element_type=jnp.float32
    )


def dot_first(left_m, right_m):
    return lax.dot_general(
        left_m, right_m, (((0,), (0,)), ((), ())), preferred_element_type=jnp.float32
    )


def norm_back(field_in, inv_scale, gain_f, grad_in):
    scaled = grad_in * gain_f
    grad_field = inv_scale * scaled - field_in * inv_scale**3 * jnp.mean(
        field_in * scaled, axis=-1, keepdims=True
    )
    grad_gain = jnp.sum(grad_in * field_in * inv_scale, axis=0)
    return (grad_field, grad_gain)


MESH = pl.DeviceIdType.MESH
VMEM_BYTES = 56 * 1024 * 1024


def parent_of(key, order):
    for place in range(len(order) - 1, -1, -1):
        if key[place]:
            return key[:place] + (key[place] - 1,) + key[place + 1 :], order[place]
    return None, None


def held(key, order, axes):
    return all(by == 0 or axis in axes for axis, by in zip(order, key))


def hop_order(items, sizes, eager):
    pace = {"z": 22.0, "y": 22.0, "x": 22.0, "c": 5.0}
    hops, below = {}, {}
    for number, (order, size, axes) in enumerate(items):
        for key in itertools.product(*[range(sizes[axis]) for axis in order]):
            if not held(key, order, axes):
                before, axis = parent_of(key, order)
                hops[(number, key)] = ((number, before), axis, size * pace[axis])
    for hop in hops:
        at = hop
        while at in hops:
            below[at] = below.get(at, 0) + hops[hop][2]
            at = hops[at][0]
    free, arrived, started = {}, {}, []
    waiting = sorted(hops)
    while waiting:
        best = None
        for hop in waiting:
            before, axis, cost = hops[hop]
            if before in hops and before not in arrived:
                continue
            start = max(free.get(axis, 0.0), arrived.get(before, 0.0))
            rank = (start, -below[hop], hop)
            if best is None or rank < best[0]:
                best = (rank, hop)
        (start, _, _), hop = best
        waiting.remove(hop)
        before, axis, cost = hops[hop]
        free[axis] = start + cost
        arrived[hop] = start + cost + 1.5
        started.append((arrived.get(before, 0.0) if eager else start, -below[hop], hop))
    started = sorted(started)
    return [(hop, hops[hop][0], hops[hop][1]) for _, _, hop in started], [at for at, _, _ in started]


def place_of(sizes):
    e_pos, t_pos = lax.axis_index("expert"), lax.axis_index("tensor")
    here = {"z": e_pos // sizes["y"], "y": e_pos % sizes["y"], "x": t_pos // sizes["c"], "c": t_pos % sizes["c"]}

    def device(coords):
        return (coords["z"] * sizes["y"] + coords["y"], coords["x"] * sizes["c"] + coords["c"])

    def moved(axis, by):
        there = dict(here)
        there[axis] = lax.rem(here[axis] + (by % sizes[axis]), sizes[axis])
        return there

    return here, device, moved


def owner_of(here, key, order, sizes):
    there = dict(here)
    for axis, by in zip(order, key):
        if by:
            there[axis] = lax.rem(here[axis] + (sizes[axis] - by), sizes[axis])
    return there


def enter(axes, moved, device, sizes):
    barrier = pltpu.get_barrier_semaphore()
    count = 0
    for axis in axes:
        for by in (1, -1) if sizes[axis] > 2 else (1,):
            pl.semaphore_signal(barrier, inc=1, device_id=device(moved(axis, by)), device_id_type=MESH)
            count += 1
    pl.semaphore_wait(barrier, count)


def part_rows(ref, start, rows):
    return ref.at[pl.ds(pl.multiple_of(start, 16), rows)]


def index_of(coords, order, sizes):
    number = 0
    for axis in "zyxc":
        if axis in order:
            number = number * sizes[axis] + coords[axis]
    return number


def held_blocks(items, sizes):
    blocks = []
    for number, (order, _, _, _, axes, _, _) in enumerate(items):
        for key in itertools.product(*[range(sizes[axis]) for axis in order]):
            if held(key, order, axes):
                blocks.append((number, key))
    return blocks


def gather_kernel(items, sizes, hops, *refs):
    n = len(items)
    ins, outs = refs[:n], refs[n : 2 * n]
    own_sem, send_sem, recv_sem = refs[2 * n :]
    here, device, moved = place_of(sizes)

    def slot(number, key):
        order, rows, pitch, base = items[number][:4]
        owner = owner_of(here, key, order, sizes)
        return part_rows(outs[number], index_of(owner, order, sizes) * pitch + base, rows)

    def source(number, key):
        order, rows, _, _, axes, pitch, base = items[number]
        if not held(key, order, axes):
            return slot(number, key)
        owner = owner_of(here, key, order, sizes)
        return part_rows(ins[number], index_of(owner, axes, sizes) * pitch + base, rows)

    place = {hop: at for at, (hop, _, _) in enumerate(hops)}

    def hop_copy(hop, src, axis, dst):
        at = place[hop]
        return pltpu.make_async_remote_copy(
            src_ref=src,
            dst_ref=dst,
            send_sem=send_sem.at[at],
            recv_sem=recv_sem.at[at],
            device_id=device(moved(axis, 1)),
            device_id_type=MESH,
        )

    own = [
        pltpu.make_async_copy(source(*block), slot(*block), own_sem.at[i])
        for i, block in enumerate(held_blocks(items, sizes))
    ]
    for copy in own:
        copy.start()
    enter(sorted({axis for _, _, axis in hops}), moved, device, sizes)
    arrived, sent = set(), []

    def await_block(hop, axis):
        if hop in place and hop not in arrived:
            arrived.add(hop)
            block = slot(*hop)
            hop_copy(hop, block, axis, block).wait_recv()

    axis_of = {hop: axis for hop, _, axis in hops}
    for hop, before, axis in hops:
        if before in place:
            await_block(before, axis_of[before])
        copy = hop_copy(hop, source(*before), axis, slot(*before))
        copy.start()
        sent.append(copy)
    for hop, _, axis in hops:
        await_block(hop, axis)
    for copy in sent:
        copy.wait_send()
    for copy in own:
        copy.wait()


def gather(arrays, plans, sizes, collective_id):
    n = len(plans)
    items = [plan[1:] for plan in plans]
    cost = [(plan[1], plan[2] * arrays[plan[0]].shape[1] * 2e-6, plan[5]) for plan in plans]
    hops, _ = hop_order(cost, sizes, True)
    ids = sorted({plan[0] for plan in plans})
    shapes = []
    for a in ids:
        rows = sum(p[2] * math.prod(sizes[axis] for axis in p[1]) for p in plans if p[0] == a)
        shapes.append(jax.ShapeDtypeStruct((rows, arrays[a].shape[1]), arrays[a].dtype))

    def kernel(*refs):
        ins = {a: refs[i] for i, a in enumerate(ids)}
        outs = {a: refs[len(ids) + i] for i, a in enumerate(ids)}
        rest = refs[2 * len(ids) :]
        gather_kernel(
            items, sizes, hops, *[ins[p[0]] for p in plans], *[outs[p[0]] for p in plans], *rest
        )

    return pl.pallas_call(
        kernel,
        out_shape=shapes,
        in_specs=[pl.BlockSpec(memory_space=pl.ANY)] * len(ids),
        out_specs=[pl.BlockSpec(memory_space=pl.ANY)] * len(ids),
        scratch_shapes=[
            pltpu.SemaphoreType.DMA((len(held_blocks(items, sizes)),)),
            pltpu.SemaphoreType.DMA((len(hops),)),
            pltpu.SemaphoreType.DMA((len(hops),)),
        ],
        compiler_params=pltpu.CompilerParams(
            collective_id=collective_id, has_side_effects=True, vmem_limit_bytes=VMEM_BYTES
        ),
    )(*[arrays[a] for a in ids])


def scatter(arrays, plans, sizes, collective_id):
    n_arrays = len(arrays)
    cost = [(order, rows * arrays[a].shape[1] * 2e-6, "") for a, order, rows, _, _ in plans]
    hops = hop_order(cost, sizes, False)[0][::-1]
    place = {hop: at for at, (hop, _, _) in enumerate(hops)}
    children = {}
    for hop, before, _ in hops:
        children.setdefault(before, []).append(hop)
    counts = {a: math.prod(sizes[axis] for axis in order) for a, order, _, _, _ in plans}
    slots, received = {}, [0] * n_arrays
    for hop, _, _ in hops:
        a, _, rows, _, _ = plans[hop[0]]
        slots[hop] = received[a]
        received[a] += rows
    shapes = [
        jax.ShapeDtypeStruct((v.shape[0] // counts[a], v.shape[1]), jnp.float32)
        for a, v in enumerate(arrays)
    ]

    def kernel(*refs):
        ins, outs = refs[:n_arrays], refs[n_arrays : 2 * n_arrays]
        parts, got = refs[2 * n_arrays : 3 * n_arrays], refs[3 * n_arrays : 4 * n_arrays]
        load_sem, send_sem, recv_sem = refs[4 * n_arrays :]
        here, device, moved = place_of(sizes)
        loads = [pltpu.make_async_copy(ins[a], parts[a], load_sem.at[a]) for a in range(n_arrays)]
        for copy in loads:
            copy.start()
        enter(sorted({axis for _, _, axis in hops}), moved, device, sizes)

        def own_start(number, key):
            _, order, _, pitch, shift = plans[number]
            owner = owner_of(here, key, order, sizes)
            return pl.multiple_of(index_of(owner, order, sizes) * pitch + shift, 16)

        def hop_copy(hop, axis):
            a, _, rows, _, _ = plans[hop[0]]
            return pltpu.make_async_remote_copy(
                src_ref=parts[a].at[pl.ds(own_start(*hop), rows)],
                dst_ref=got[a].at[pl.ds(slots[hop], rows)],
                send_sem=send_sem.at[place[hop]],
                recv_sem=recv_sem.at[place[hop]],
                device_id=device(moved(axis, -1)),
                device_id_type=MESH,
            )

        axis_of = {hop: axis for hop, _, axis in hops}
        loaded = set()

        def summed(number, key):
            a, _, rows, _, _ = plans[number]
            if a not in loaded:
                loaded.add(a)
                loads[a].wait()
            return a, rows, own_start(number, key), children.get((number, key), [])

        sent = []
        for hop, before, axis in hops:
            a, rows, start, below = summed(*hop)
            for child in below:
                hop_copy(child, axis_of[child]).wait_recv()
            if below:
                step = 16
                ref, buf = parts[a], got[a]

                @pl.loop(0, rows // step)
                def _(i, ref=ref, buf=buf, start=start, below=below):
                    at = pl.ds(pl.multiple_of(start + i * step, 16), step)
                    total = ref[at, :].astype(jnp.float32)
                    for child in below:
                        more = pl.ds(pl.multiple_of(slots[child] + i * step, 16), step)
                        total = total + buf[more, :].astype(jnp.float32)
                    ref[at, :] = total.astype(ref.dtype)

            copy = hop_copy(hop, axis)
            copy.start()
            sent.append(copy)
        for number, (a, order, rows, pitch, shift) in enumerate(plans):
            key = (0,) * len(order)
            a, rows, start, below = summed(number, key)
            for child in below:
                hop_copy(child, axis_of[child]).wait_recv()
            step = 16
            ref, buf, out = parts[a], got[a], outs[a]

            @pl.loop(0, rows // step)
            def _(i, ref=ref, buf=buf, out=out, start=start, below=below, shift=shift):
                total = ref[pl.ds(pl.multiple_of(start + i * step, 16), step), :].astype(jnp.float32)
                for child in below:
                    more = pl.ds(pl.multiple_of(slots[child] + i * step, 16), step)
                    total = total + buf[more, :].astype(jnp.float32)
                out[pl.ds(pl.multiple_of(shift + i * step, 16), step), :] = total

        for copy in sent:
            copy.wait_send()

    return pl.pallas_call(
        kernel,
        out_shape=shapes,
        in_specs=[pl.BlockSpec(memory_space=pl.ANY)] * n_arrays,
        out_specs=[pl.BlockSpec(memory_space=pltpu.VMEM)] * n_arrays,
        scratch_shapes=[pltpu.VMEM(v.shape, v.dtype) for v in arrays]
        + [pltpu.VMEM((max(received[a], 16), v.shape[1]), v.dtype) for a, v in enumerate(arrays)]
        + [
            pltpu.SemaphoreType.DMA((n_arrays,)),
            pltpu.SemaphoreType.DMA((len(hops),)),
            pltpu.SemaphoreType.DMA((len(hops),)),
        ],
        compiler_params=pltpu.CompilerParams(
            collective_id=collective_id, has_side_effects=True, vmem_limit_bytes=VMEM_BYTES
        ),
    )(*arrays)


SIZES = {"z": 4, "y": 2, "x": 2, "c": 2}


def direct():
    return lax.axis_size("expert") == 8 and lax.axis_size("tensor") == 4


def halves(a, order_a, order_b, rows):
    return [(a, order_a, rows // 2, rows, 0), (a, order_b, rows // 2, rows, rows // 2)]


def gather_tensor(part, collective_id):
    if not direct():
        return lax.all_gather(part, "tensor", axis=0, tiled=True)
    plans = [plan + ("", 0, plan[4]) for plan in halves(0, "xc", "xc", part.shape[0])]
    return gather([part], plans, SIZES, collective_id)[0]


def scatter_tensor(whole, collective_id):
    if not direct():
        part = lax.psum_scatter(whole, "tensor", scatter_dimension=0, tiled=True)
        return part.astype(jnp.float32)
    return scatter([whole], halves(0, "xc", "xc", whole.shape[0] // 4), SIZES, collective_id)[0]


def slot_events(items, sizes, chunk_of, n_chunks, per_chunk, reverse, tau=1.6):
    speed = {"z": 1.0, "y": 1.0, "x": 1.0, "c": 5.0}
    hops = {}
    for number, (order, cost) in enumerate(items):
        for key in itertools.product(*[range(sizes[axis]) for axis in order]):
            before, axis = parent_of(key, order)
            if before is not None:
                hops[(number, key)] = ((number, before), axis, cost / speed[axis])
    children, depth = {}, {}
    for hop, (before, _, _) in hops.items():
        children.setdefault(before, []).append(hop)
    for hop in hops:
        at = hop
        while at in hops:
            if reverse:
                depth[hop] = depth.get(hop, 0) + hops[at][2]
            else:
                depth[at] = depth.get(at, 0) + hops[hop][2]
            at = hops[at][0]
    free, arrived, now = {}, {}, 8.0
    waiting = sorted(hops, key=lambda hop: (-depth[hop], hop))
    events = [[] for _ in range(n_chunks * per_chunk + 1)]

    def needs(hop):
        if reverse:
            return children.get(hop, [])
        return [hops[hop][0]] if hops[hop][0] in hops else []

    def start_ready(slot, computed):
        for hop in list(waiting):
            if reverse and chunk_of(*hop) >= computed:
                continue
            if all(other in arrived and arrived[other] <= now for other in needs(hop)):
                waiting.remove(hop)
                _, axis, cost = hops[hop]
                begin = max(free.get(axis, 0.0), now)
                free[axis] = begin + cost
                arrived[hop] = begin + cost + 2.0
                events[slot].append(hop)

    for chunk in range(n_chunks):
        for part in range(per_chunk):
            slot = chunk * per_chunk + part
            start_ready(slot, chunk)
            if part == 0 and not reverse:
                blocks = [hop for hop in hops if chunk_of(*hop) == chunk]
                while not all(hop in arrived and arrived[hop] <= now for hop in blocks):
                    now = min(t for t in arrived.values() if t > now)
                    start_ready(slot, chunk)
            now += tau
    while waiting:
        start_ready(n_chunks * per_chunk, n_chunks)
        if waiting:
            now = min(t for t in arrived.values() if t > now)
    axis_of = {hop: hops[hop][1] for hop in hops}
    before_of = {hop: hops[hop][0] for hop in hops}
    return events, axis_of, before_of, children


ORDERS = ("zyxc", "zxyc")
CHUNK = 256
PER = 3


def chunk_number(reverse):
    def of(number, key):
        coord = dict(zip(ORDERS[number], key))
        if reverse:
            return (3 - coord["z"]) * 4 + (1 - coord["y"]) * 2 + number
        return coord["z"] * 4 + coord["y"] * 2 + number

    return of


def chunk_start(step, here, half_rows, reverse):
    dz, dy, half = step // 4, (step // 2) % 2, step % 2
    if reverse:
        dz, dy = 3 - dz, 1 - dy
    z, y = lax.rem(here["z"] + 4 - dz, 4), lax.rem(here["y"] + 2 - dy, 2)
    return pl.multiple_of(half * half_rows + (z * 2 + y) * CHUNK, CHUNK)


def run_events(events, step, part, act):
    for chunk in range((len(events) - 1) // PER):
        todo = events[chunk * PER + part]
        if todo:

            @pl.when(step == chunk)
            def _(todo=todo):
                act(todo)


def weight_copies(gate, up, down, shared, w_gate_up, w_down, segments, sem):
    n_routed, units, _ = gate.shape
    n_from, _, shared_units, cols = shared.shape
    total = sum(segments)
    copies = []
    for which, (src, dst, base) in enumerate(
        [(gate, w_gate_up, 0), (up, w_gate_up, total), (down, w_down, 0)]
    ):
        for i in range(n_routed):
            start = base + sum(segments[:i])
            copies.append((src.at[i], dst.at[pl.ds(start, units)]))
            dst[start + units : start + segments[i], :] = jnp.zeros(
                (segments[i] - units, dst.shape[1]), dst.dtype
            )
        start = base + sum(segments[:-1])
        for i in range(n_from):
            copies.append(
                (shared.at[i, which], dst.at[pl.ds(start, shared_units), pl.ds(i * cols, cols)])
            )
        dst[start + shared_units : start + segments[-1], :] = jnp.zeros(
            (segments[-1] - shared_units, dst.shape[1]), dst.dtype
        )
    return [pltpu.make_async_copy(src, dst, sem.at[i]) for i, (src, dst) in enumerate(copies)]


def n_weight_copies(gate, shared):
    return 3 * (gate.shape[0] + shared.shape[0])


def dot_nt(left, right):
    return lax.dot_general(left, right, (((1,), (1,)), ((), ())), preferred_element_type=jnp.float32)


def mixture_forward(normed_mid, dy_all, mask_all, weights_w, router_w, here_units, collective_id):
    sizes = SIZES
    part_rows_n, width = normed_mid.shape
    block = part_rows_n // 2
    n_rows = part_rows_n * 32
    half_rows = n_rows // 2
    units = sum(here_units)
    n_chunks = n_rows // CHUNK
    seg = here_units
    n_copies = n_weight_copies(weights_w[0], weights_w[3])
    n_routed = len(seg) - 1
    events, axis_of, before_of, _ = slot_events(
        [(order, 8.0) for order in ORDERS], sizes, chunk_number(False), n_chunks, PER, False
    )
    place = {hop: at for at, hop in enumerate(sorted(axis_of))}
    bf = jnp.bfloat16
    arrived, actions = set(), []
    for number, todo in enumerate(events):
        actions.append([])
        needed = [(before_of[hop], hop) for hop in todo]
        if number % PER == 0 and number < n_chunks * PER:
            mine = [hop for hop in axis_of if chunk_number(False)(*hop) == number // PER]
            needed += [(hop, None) for hop in sorted(mine)]
        for block_key, hop in needed:
            if block_key in axis_of and block_key not in arrived:
                arrived.add(block_key)
                actions[-1].append((block_key, True))
            if hop is not None:
                actions[-1].append((hop, False))

    def kernel(
        nm, dy, mask, gate_h, up_h, down_h, shared_h, router_h,
        x_out, hid_out, dgu_out, gg,
        x_vm, wgu, wd, wr, dy_buf, hid_st, dgu_st,
        w_sem, own_sem, dy_sem, x_sem, st_sem, send_sem, recv_sem,
    ):
        here, device, moved = place_of(sizes)
        e_pos = lax.axis_index("expert")

        def slot(number, key):
            owner = owner_of(here, key, ORDERS[number], sizes)
            start = number * half_rows + index_of(owner, "zyxc", sizes) * block
            return x_vm.at[pl.ds(pl.multiple_of(start, block), block)]

        def source(number, key):
            if any(key):
                return slot(number, key)
            return nm.at[pl.ds(number * block, block)]

        def hop_copy(hop, src, dst):
            return pltpu.make_async_remote_copy(
                src_ref=src,
                dst_ref=dst,
                send_sem=send_sem.at[place[hop]],
                recv_sem=recv_sem.at[place[hop]],
                device_id=device(moved(axis_of[hop], 1)),
                device_id_type=MESH,
            )

        weights = weight_copies(gate_h, up_h, down_h, shared_h, wgu, wd, seg, w_sem)
        weights.append(pltpu.make_async_copy(router_h, wr, w_sem.at[n_copies]))
        own = [
            pltpu.make_async_copy(source(i, (0,) * 4), slot(i, (0,) * 4), own_sem.at[i]) for i in range(2)
        ]

        def dy_copy(step):
            at = chunk_start(step, here, half_rows, False)
            return pltpu.make_async_copy(
                dy.at[pl.ds(at, CHUNK)], dy_buf.at[lax.rem(step, 2)], dy_sem.at[lax.rem(step, 2)]
            )

        def x_copy(step):
            at = chunk_start(step, here, half_rows, False)
            return pltpu.make_async_copy(x_vm.at[pl.ds(at, CHUNK)], x_out.at[pl.ds(at, CHUNK)], x_sem.at[step])

        def st_copies(step):
            at = chunk_start(step, here, half_rows, False)
            turn = lax.rem(step, 2)
            return [
                pltpu.make_async_copy(st.at[turn], out.at[pl.ds(at, CHUNK)], st_sem.at[i, turn])
                for i, (st, out) in enumerate([(hid_st, hid_out), (dgu_st, dgu_out)])
            ]

        for copy in own + weights:
            copy.start()
        dy_copy(0).start()
        enter("zyxc", moved, device, sizes)

        def act(todo):
            for hop, wait in todo:
                if wait:
                    hop_copy(hop, slot(*hop), slot(*hop)).wait_recv()
                else:
                    hop_copy(hop, source(*before_of[hop]), slot(*before_of[hop])).start()

        @pl.loop(0, n_chunks)
        def _(step):
            for chunk in range(n_chunks):

                @pl.when(step == chunk)
                def _(chunk=chunk):
                    act(actions[chunk * PER])
                    if chunk == 0:
                        for copy in own + weights:
                            copy.wait()

            turn = lax.rem(step, 2)
            at = chunk_start(step, here, half_rows, False)
            rows = pl.ds(at, CHUNK)
            x_copy(step).start()
            dy_copy(step).wait()

            @pl.when(step + 1 < n_chunks)
            def _():
                dy_copy(step + 1).start()

            logits = jnp.dot(x_vm[rows, :], wr[...], preferred_element_type=jnp.float32)
            chosen = jax.nn.sigmoid(logits) * mask[rows, :].astype(jnp.float32)
            gate_weights = ROUTE_SCALE * chosen / jnp.sum(chosen, axis=1, keepdims=True)
            lane = lax.broadcasted_iota(jnp.int32, (CHUNK, 128), 1)
            scales = []
            for which in range(n_routed):
                mine = jnp.where(lane == e_pos * n_routed + which, gate_weights, 0.0)
                scales.append(jnp.sum(mine, axis=1, keepdims=True))

            @pl.when(step >= 2)
            def _():
                for copy in st_copies(step - 2):
                    copy.wait()

            sums = [jnp.zeros((CHUNK, 128), jnp.float32) for _ in range(n_routed)]
            ends = [sum(seg[: i + 1]) for i in range(len(seg))]
            for number, begin in enumerate(range(0, units, 256)):
                end = min(begin + 256, units)
                g_tile = dot_nt(x_vm[rows, :], wgu[begin:end, :])
                u_tile = dot_nt(x_vm[rows, :], wgu[units + begin : units + end, :])
                h_tile = dot_nt(dy_buf[turn], wd[begin:end, :])
                for at_lane in range(begin, end, 128):
                    which = sum(at_lane >= stop for stop in ends)
                    part = slice(at_lane - begin, at_lane - begin + 128)
                    cols = slice(at_lane, at_lane + 128)
                    more = slice(units + at_lane, units + at_lane + 128)
                    g, u, h = g_tile[:, part], u_tile[:, part], h_tile[:, part]
                    sig = jax.nn.sigmoid(g)
                    silu = g * sig
                    hid = silu * u
                    if which < n_routed:
                        sums[which] = sums[which] + h * hid
                        hid = hid * scales[which]
                        h = h * scales[which]
                    hid_st[turn, :, cols] = hid.astype(bf)
                    dgu_st[turn, :, cols] = (h * u * (sig + silu * (1.0 - sig))).astype(bf)
                    dgu_st[turn, :, more] = (h * silu).astype(bf)
                if number == 1:
                    run_events(actions, step, 1, act)
                    run_events(actions, step, 2, act)

            total = jnp.zeros((CHUNK, 128), jnp.float32)
            for which in range(n_routed):
                mine = jnp.sum(sums[which], axis=1, keepdims=True)
                total = jnp.where(lane == e_pos * n_routed + which, mine, total)
            gg[rows, :] = total.astype(bf)

            for copy in st_copies(step):
                copy.start()

        for step in range(n_chunks):
            x_copy(step).wait()
        for step in (n_chunks - 2, n_chunks - 1):
            for copy in st_copies(step):
                copy.wait()
        for hop in sorted(axis_of):
            hop_copy(hop, source(*before_of[hop]), slot(*before_of[hop])).wait_send()

    any_spec, vm_spec = pl.BlockSpec(memory_space=pl.ANY), pl.BlockSpec(memory_space=pltpu.VMEM)
    return pl.pallas_call(
        kernel,
        out_shape=[
            jax.ShapeDtypeStruct((n_rows, width), bf),
            jax.ShapeDtypeStruct((n_rows, units), bf),
            jax.ShapeDtypeStruct((n_rows, 2 * units), bf),
            jax.ShapeDtypeStruct((n_rows, 128), bf),
        ],
        in_specs=[any_spec, any_spec, vm_spec] + [any_spec] * 5,
        out_specs=[any_spec] * 3 + [vm_spec],
        scratch_shapes=[
            pltpu.VMEM((n_rows, width), bf),
            pltpu.VMEM((2 * units, width), bf),
            pltpu.VMEM((units, width), bf),
            pltpu.VMEM((width, 128), bf),
            pltpu.VMEM((2, CHUNK, width), bf),
            pltpu.VMEM((2, CHUNK, units), bf),
            pltpu.VMEM((2, CHUNK, 2 * units), bf),
            pltpu.SemaphoreType.DMA((n_copies + 1,)),
            pltpu.SemaphoreType.DMA((2,)),
            pltpu.SemaphoreType.DMA((2,)),
            pltpu.SemaphoreType.DMA((n_chunks,)),
            pltpu.SemaphoreType.DMA((2, 2)),
            pltpu.SemaphoreType.DMA((len(axis_of),)),
            pltpu.SemaphoreType.DMA((len(axis_of),)),
        ],
        compiler_params=pltpu.CompilerParams(
            collective_id=collective_id, has_side_effects=True, vmem_limit_bytes=VMEM_BYTES
        ),
    )(normed_mid, dy_all, mask_all, *weights_w, router_w)


def mixture_backward(hidden, grad_gate_up, gate_sums, residual, weights_w, here_units, collective_id):
    sizes = SIZES
    n_rows, units = hidden.shape
    width = weights_w[0].shape[2]
    n_copies = n_weight_copies(weights_w[0], weights_w[3])
    all_width = width + 128
    half_rows = n_rows // 2
    block = n_rows // 64
    n_chunks = n_rows // CHUNK
    events, axis_of, before_of, children = slot_events(
        [(order, 6.9) for order in ORDERS], sizes, chunk_number(True), n_chunks, PER, True
    )
    place = {hop: at for at, hop in enumerate(sorted(axis_of))}
    bf = jnp.bfloat16
    tile_n = width // 4

    def kernel(
        hid_in, dgu_in, gg_in, resid, gate_h, up_h, down_h, shared_h,
        sums, x_out, unit_out,
        parts, got, wgu, wd, hid_b, dgu_b, gg_b, x_st, unit_st,
        w_sem, in_sem, x_sem, unit_sem, send_sem, recv_sem,
    ):
        here, device, moved = place_of(sizes)

        def own_start(number, key):
            owner = owner_of(here, key, ORDERS[number], sizes)
            return pl.multiple_of(number * half_rows + index_of(owner, "zyxc", sizes) * block, block)

        def hop_copy(hop):
            return pltpu.make_async_remote_copy(
                src_ref=parts.at[pl.ds(own_start(*hop), block)],
                dst_ref=got.at[pl.ds(place[hop] * block, block)],
                send_sem=send_sem.at[place[hop]],
                recv_sem=recv_sem.at[place[hop]],
                device_id=device(moved(axis_of[hop], -1)),
                device_id_type=MESH,
            )

        def total_of(number, key, write):
            below = children.get((number, key), [])
            for child in below:
                hop_copy(child).wait_recv()
            start = own_start(number, key)
            tile = 16

            @pl.loop(0, block // tile)
            def _(i):
                at = pl.ds(pl.multiple_of(start + i * tile, tile), tile)
                total = parts[at, :].astype(jnp.float32)
                for child in below:
                    more = pl.ds(pl.multiple_of(place[child] * block + i * tile, tile), tile)
                    total = total + got[more, :].astype(jnp.float32)
                write(i * tile, at, total)

        def keep(offset, at, total):
            parts[at, :] = total.astype(bf)

        def act(todo):
            for hop in todo:
                if children.get(hop):
                    total_of(*hop, keep)
                hop_copy(hop).start()

        weights = weight_copies(gate_h, up_h, down_h, shared_h, wgu, wd, here_units, w_sem)

        def in_copies(step):
            at = pl.ds(chunk_start(step, here, half_rows, True), CHUNK)
            turn = lax.rem(step, 2)
            return [
                pltpu.make_async_copy(src.at[at], dst.at[turn], in_sem.at[i, turn])
                for i, (src, dst) in enumerate([(dgu_in, dgu_b), (hid_in, hid_b), (gg_in, gg_b)])
            ]

        def x_copy(step):
            turn, half = lax.rem(step, 2), step % 2
            at = (chunk_start(step, here, half_rows, True) - half * half_rows) // CHUNK
            return pltpu.make_async_copy(x_st.at[turn], x_out.at[at, :, :, half], x_sem.at[turn])

        def unit_copy(step):
            at = pl.ds(chunk_start(step, here, half_rows, True), CHUNK)
            turn = lax.rem(step, 2)
            return pltpu.make_async_copy(unit_st.at[turn], unit_out.at[:, at], unit_sem.at[turn])

        for copy in in_copies(0) + weights:
            copy.start()
        enter("zyxc", moved, device, sizes)
        for copy in weights:
            copy.wait()

        @pl.loop(0, n_chunks)
        def _(step):
            turn = lax.rem(step, 2)
            at = chunk_start(step, here, half_rows, True)
            rows = pl.ds(at, CHUNK)
            run_events(events, step, 0, act)
            for copy in in_copies(step):
                copy.wait()

            @pl.when(step + 1 < n_chunks)
            def _():
                for copy in in_copies(step + 1):
                    copy.start()

            @pl.when(step >= 2)
            def _():
                unit_copy(step - 2).wait()

            for part in range(2):
                for n in range(part * units, (part + 1) * units, 128):
                    unit_st[turn, n : n + 128, :] = dgu_b[turn, :, n : n + 128].T
                for n in range(part * (width // 2), (part + 1) * (width // 2), tile_n):
                    cols = slice(n, n + tile_n)
                    total = jnp.dot(dgu_b[turn], wgu[:, cols], preferred_element_type=jnp.float32)
                    parts[rows, cols] = total.astype(bf)
                if part == 0:
                    run_events(events, step, 1, act)
            parts[rows, width:] = gg_b[turn]
            run_events(events, step, 2, act)

            @pl.when(step >= 2)
            def _():
                x_copy(step - 2).wait()

            for n in range(0, units, 128):
                unit_st[turn, 2 * units + n : 2 * units + n + 128, :] = hid_b[turn, :, n : n + 128].T
            for n in range(0, width, tile_n):
                cols = slice(n, n + tile_n)
                total = jnp.dot(hid_b[turn], wd[:, cols], preferred_element_type=jnp.float32)
                x_st[turn, n // tile_n] = total.astype(bf).reshape(CHUNK // block, block, tile_n)

            @pl.when(step >= n_chunks - 2)
            def _():
                own = lax.axis_index("tensor")
                for n in range(0, width, tile_n):
                    more = resid[pl.ds(pl.multiple_of(lax.rem(step, 2) * block, block), block), n : n + tile_n]
                    total = x_st[turn, n // tile_n, own].astype(jnp.float32) + more
                    x_st[turn, n // tile_n, own] = total.astype(bf)

            x_copy(step).start()
            unit_copy(step).start()

        act(events[-1])
        for number in range(2):

            def give(offset, at, total, number=number):
                sums[pl.ds(pl.multiple_of(number * block + offset, 16), 16), :] = total

            total_of(number, (0,) * 4, give)
        for step in (n_chunks - 2, n_chunks - 1):
            x_copy(step).wait()
            unit_copy(step).wait()
        for hop in sorted(axis_of):
            hop_copy(hop).wait_send()

    any_spec, vm_spec = pl.BlockSpec(memory_space=pl.ANY), pl.BlockSpec(memory_space=pltpu.VMEM)
    n_hops = len(axis_of)
    return pl.pallas_call(
        kernel,
        out_shape=[
            jax.ShapeDtypeStruct((2 * block, all_width), jnp.float32),
            jax.ShapeDtypeStruct(
                (half_rows // CHUNK, width // tile_n, CHUNK // block, 2, block, tile_n), bf
            ),
            jax.ShapeDtypeStruct((3 * units, n_rows), bf),
        ],
        in_specs=[any_spec] * 3 + [vm_spec] + [any_spec] * 4,
        out_specs=[vm_spec, any_spec, any_spec],
        scratch_shapes=[
            pltpu.VMEM((n_rows, all_width), bf),
            pltpu.VMEM((n_hops * block, all_width), bf),
            pltpu.VMEM((2 * units, width), bf),
            pltpu.VMEM((units, width), bf),
            pltpu.VMEM((2, CHUNK, units), bf),
            pltpu.VMEM((2, CHUNK, 2 * units), bf),
            pltpu.VMEM((2, CHUNK, 128), bf),
            pltpu.VMEM((2, width // tile_n, CHUNK // block, block, tile_n), bf),
            pltpu.VMEM((2, 3 * units, CHUNK), bf),
            pltpu.SemaphoreType.DMA((n_copies,)),
            pltpu.SemaphoreType.DMA((3, 2)),
            pltpu.SemaphoreType.DMA((2,)),
            pltpu.SemaphoreType.DMA((2,)),
            pltpu.SemaphoreType.DMA((n_hops,)),
            pltpu.SemaphoreType.DMA((n_hops,)),
        ],
        compiler_params=pltpu.CompilerParams(
            collective_id=collective_id, has_side_effects=True, vmem_limit_bytes=VMEM_BYTES
        ),
    )(hidden, grad_gate_up, gate_sums, residual, *weights_w)


def final_sums(parts_in, plans, unit_rows, x_all, dy_all, here_units, n_routed, units, shared_units, collective_id):
    sizes = SIZES
    n_arrays = len(parts_in)
    n_rows, width = x_all.shape
    total_units = sum(here_units)
    slab = 256
    n_slabs = width // slab
    sh_pad = -(-shared_units // 16) * 16
    n_steps = 2 * n_slabs
    bf = jnp.bfloat16
    events, axis_of, before_of, children = slot_events(
        [(order, rows * parts_in[a].shape[1] * 44e-6) for a, order, rows, _, _ in plans],
        sizes,
        lambda number, key: -1,
        n_steps,
        1,
        True,
        8.0,
    )
    place = {hop: at for at, hop in enumerate(sorted(axis_of))}
    counts = {a: math.prod(sizes[axis] for axis in order) for a, order, _, _, _ in plans}
    slots, received = {}, [0] * n_arrays
    for hop in sorted(axis_of):
        a, _, rows, _, _ = plans[hop[0]]
        slots[hop] = received[a]
        received[a] += rows

    def kernel(*refs):
        refs = list(refs)

        def take(n):
            got = refs[:n]
            del refs[:n]
            return got

        ins, (unit_h, x_h, dy_h) = take(n_arrays), take(3)
        outs, (g_out, u_out, d_out), sh_outs = take(n_arrays), take(3), take(3)
        parts, got = take(n_arrays), take(n_arrays)
        slab_buf, unit_t, st, sh_st, sh_got = take(5)
        load_sem, unit_sem, slab_sem, st_sem, send_sem, recv_sem, sh_send, sh_recv = refs
        e_pos, t_pos = lax.axis_index("expert"), lax.axis_index("tensor")
        here, device, moved = place_of(sizes)
        loads = [pltpu.make_async_copy(ins[a], parts[a], load_sem.at[a]) for a in range(n_arrays)]

        def own_start(number, key):
            _, order, _, pitch, base = plans[number]
            owner = owner_of(here, key, order, sizes)
            return pl.multiple_of(index_of(owner, order, sizes) * pitch + base, 16)

        def hop_copy(hop):
            a, _, rows, _, _ = plans[hop[0]]
            return pltpu.make_async_remote_copy(
                src_ref=parts[a].at[pl.ds(own_start(*hop), rows)],
                dst_ref=got[a].at[pl.ds(slots[hop], rows)],
                send_sem=send_sem.at[place[hop]],
                recv_sem=recv_sem.at[place[hop]],
                device_id=device(moved(axis_of[hop], -1)),
                device_id_type=MESH,
            )

        def total_of(number, key, write):
            a, _, rows, _, _ = plans[number]
            below = children.get((number, key), [])
            for child in below:
                hop_copy(child).wait_recv()
            start = own_start(number, key)

            @pl.loop(0, rows // 16)
            def _(i):
                at = pl.ds(pl.multiple_of(start + i * 16, 16), 16)
                total = parts[a][at, :].astype(jnp.float32)
                for child in below:
                    more = pl.ds(pl.multiple_of(slots[child] + i * 16, 16), 16)
                    total = total + got[a][more, :].astype(jnp.float32)
                write(a, i * 16, at, total)

        def keep(a, offset, at, total):
            parts[a][at, :] = total.astype(bf)

        def act(todo):
            for hop in todo:
                if children.get(hop):
                    total_of(*hop, keep)
                hop_copy(hop).start()

        def run(step, first, count):
            for number in range(first, first + count):
                if events[number] and number:

                    @pl.when(step == number - first)
                    def _(number=number):
                        act(events[number])

        def slab_copy(src, number, turn, cols=slab):
            start = number * slab
            if not isinstance(number, int):
                start = pl.multiple_of(start, slab)
            return pltpu.make_async_copy(
                src.at[:, pl.ds(start, cols)], slab_buf.at[turn, :, pl.ds(0, cols)], slab_sem.at[turn]
            )

        shared_rows = sum(here_units[:-1])

        def sh_copy(which, to, src):
            return pltpu.make_async_remote_copy(
                src_ref=sh_st.at[which, to],
                dst_ref=sh_got.at[which, src],
                send_sem=sh_send.at[which, to],
                recv_sem=sh_recv.at[which, src],
                device_id=(to, t_pos),
                device_id_type=MESH,
            )

        def give_shared(which, step, part):
            @pl.when(step == e_pos)
            def _():
                sh_got[which, step] = part

            @pl.when(step != e_pos)
            def _():
                sh_st[which, step] = part
                sh_copy(which, step, e_pos).start()

        unit_load = pltpu.make_async_copy(unit_h, unit_t, unit_sem)
        for copy in loads:
            copy.start()
        barrier = pltpu.get_barrier_semaphore()
        n_expert = sizes["z"] * sizes["y"]
        others = [(lax.rem(e_pos + i, n_expert), t_pos) for i in range(1, n_expert)]
        others += [device(moved(axis, 1)) for axis in "xc"]
        for other in others:
            pl.semaphore_signal(barrier, inc=1, device_id=other, device_id_type=MESH)
        pl.semaphore_wait(barrier, len(others))
        for copy in loads:
            copy.wait()
        act(events[0])
        unit_load.start()
        slab_copy(x_h, 0, 0).start()
        unit_load.wait()

        def st_copies(turn, which, number):
            cols = pl.ds(pl.multiple_of(number * slab, slab), slab)
            out = (g_out, u_out, d_out)[which]
            pairs = [
                (st.at[turn, pl.ds(sum(here_units[:i]), units)], out.at[i, :, cols])
                for i in range(n_routed)
            ]
            return [pltpu.make_async_copy(src, dst, st_sem.at[turn, i]) for i, (src, dst) in enumerate(pairs)]

        @pl.loop(0, n_slabs)
        def _(step):
            run(step, 0, n_slabs)
            turn = lax.rem(step, 2)
            slab_copy(x_h, step, turn).wait()

            @pl.when(step + 1 < n_slabs)
            def _():
                slab_copy(x_h, step + 1, 1 - turn).start()

            @pl.when(step + 1 == n_slabs)
            def _():
                slab_copy(dy_h, 0, 1 - turn).start()

            for which in range(2):

                @pl.when(step >= 1)
                def _(which=which):
                    for copy in st_copies(which, which, step - 1):
                        copy.wait()

                st[which] = jnp.dot(
                    unit_t[which * total_units : (which + 1) * total_units, :],
                    slab_buf[turn],
                    preferred_element_type=jnp.float32,
                )
                for copy in st_copies(which, which, step):
                    copy.start()
                give_shared(which, step, st[which, shared_rows : shared_rows + sh_pad, :].astype(bf))

        for which in range(2):
            for copy in st_copies(which, which, n_slabs - 1):
                copy.wait()

        @pl.loop(0, n_slabs)
        def _(step):
            run(step, n_slabs, n_slabs)
            turn = lax.rem(step + n_slabs, 2)
            slab_copy(dy_h, step, turn).wait()

            @pl.when(step + 1 < n_slabs)
            def _():
                slab_copy(dy_h, step + 1, 1 - turn).start()

            half = lax.rem(step, 2)

            @pl.when(step >= 2)
            def _():
                for copy in st_copies(half, 2, step - 2):
                    copy.wait()

            st[half] = jnp.dot(
                unit_t[2 * total_units :, :], slab_buf[turn], preferred_element_type=jnp.float32
            )
            for copy in st_copies(half, 2, step):
                copy.start()
            give_shared(2, step, st[half, shared_rows : shared_rows + sh_pad, :].astype(bf))

        act(events[-1])
        for number, (_, order_n, _, _, base_n) in enumerate(plans):

            def give(a, offset, at, total, base_n=base_n):
                outs[a][pl.ds(pl.multiple_of(base_n + offset, 16), 16), :] = total

            total_of(number, (0,) * len(order_n), give)
        for which in range(3):
            for i in range(1, n_expert):
                other = lax.rem(e_pos + i, n_expert)
                sh_copy(which, other, other).wait_recv()
            for i in range(n_expert):
                sh_outs[which][i * shared_units : (i + 1) * shared_units, :] = sh_got[
                    which, i, :shared_units, :
                ].astype(jnp.float32)
            for i in range(1, n_expert):
                other = lax.rem(e_pos + i, n_expert)
                sh_copy(which, other, other).wait_send()
        for step in (n_slabs - 2, n_slabs - 1):
            for copy in st_copies(step % 2, 2, step):
                copy.wait()
        for hop in sorted(axis_of):
            hop_copy(hop).wait_send()

    f32 = jnp.float32
    shapes = [
        jax.ShapeDtypeStruct((v.shape[0] // counts[a], v.shape[1]), f32) for a, v in enumerate(parts_in)
    ]
    shapes += [jax.ShapeDtypeStruct((n_routed, units, width), f32)] * 3
    shapes += [jax.ShapeDtypeStruct((8 * shared_units, slab), f32)] * 3
    any_spec, vm_spec = pl.BlockSpec(memory_space=pl.ANY), pl.BlockSpec(memory_space=pltpu.VMEM)
    n_hops = len(axis_of)
    return pl.pallas_call(
        kernel,
        out_shape=shapes,
        in_specs=[any_spec] * (n_arrays + 3),
        out_specs=[vm_spec] * n_arrays + [any_spec] * 3 + [vm_spec] * 3,
        scratch_shapes=[pltpu.VMEM(v.shape, v.dtype) for v in parts_in]
        + [pltpu.VMEM((received[a], v.shape[1]), v.dtype) for a, v in enumerate(parts_in)]
        + [
            pltpu.VMEM((2, n_rows, slab), bf),
            pltpu.VMEM((3 * total_units, n_rows), bf),
            pltpu.VMEM((2, total_units, slab), f32),
            pltpu.VMEM((3, 8, sh_pad, slab), bf),
            pltpu.VMEM((3, 8, sh_pad, slab), bf),
            pltpu.SemaphoreType.DMA((n_arrays,)),
            pltpu.SemaphoreType.DMA,
            pltpu.SemaphoreType.DMA((2,)),
            pltpu.SemaphoreType.DMA((2, n_routed)),
            pltpu.SemaphoreType.DMA((n_hops,)),
            pltpu.SemaphoreType.DMA((n_hops,)),
            pltpu.SemaphoreType.DMA((3, 8)),
            pltpu.SemaphoreType.DMA((3, 8)),
        ],
        compiler_params=pltpu.CompilerParams(
            collective_id=collective_id, has_side_effects=True, vmem_limit_bytes=VMEM_BYTES
        ),
    )(*parts_in, unit_rows, x_all, dy_all)


def masked_scores(qn_blk, qr_blk, key_nope, key_rope, seg_blk, seg_ids, first_row):
    block_len = qn_blk.shape[0]
    scores = jnp.einsum("qhd,khd->hqk", qn_blk, key_nope, preferred_element_type=jnp.float32)
    scores = scores + jnp.einsum(
        "qhd,kd->hqk", qr_blk, key_rope, preferred_element_type=jnp.float32
    )
    scores = scores * (NOPE + ROPE) ** (-0.5)
    row_pos = first_row + jnp.arange(block_len, dtype=jnp.int32)
    col_pos = jnp.arange(key_nope.shape[0], dtype=jnp.int32)
    allowed = (seg_blk[:, None] == seg_ids[None, :]) & (row_pos[:, None] >= col_pos[None, :])
    return jnp.where(allowed[None], scores, NEG)


def local(
    tokens,
    segments,
    routes,
    cotangent,
    norm_in,
    w_query,
    w_latent,
    norm_latent,
    w_keyval,
    w_out,
    norm_mid,
    w_router,
    shared_gate,
    shared_up,
    shared_down,
    expert_gate,
    expert_up,
    expert_down,
):
    seq_len = tokens.shape[0]
    n_expert = lax.axis_size("expert")
    n_tensor = lax.axis_size("tensor")
    expert_pos = lax.axis_index("expert")
    tensor_pos = lax.axis_index("tensor")
    experts_all = w_router.shape[1]
    experts_here = expert_gate.shape[0]
    rows_part = seq_len // n_tensor
    both = ("expert", "tensor")

    def my_rows(whole):
        return lax.dynamic_slice_in_dim(whole, tensor_pos * rows_part, rows_part, 0)

    expert_ids = jnp.arange(experts_all, dtype=jnp.int32)
    routed = jnp.any(routes[:, :, None] == expert_ids[None, None, :], axis=1).astype(jnp.bfloat16)
    my_routed = my_rows(routed)

    n_gain, n_lat = norm_in.shape[0], norm_latent.shape[0]
    small = jnp.concatenate([norm_in, norm_mid, norm_latent, w_router.reshape(-1)])
    if direct():
        rows = -(-small.shape[0] // 2048) * 16
        small = jnp.pad(small, (0, rows * 128 - small.shape[0])).reshape(rows, 128)
        routed = routed.reshape(-1, 128)
        arrays = [small, w_query, w_keyval, w_out, routed, w_latent.T, cotangent]
        plans = [
            (a, "yz" if a == 3 else "zy", v.shape[0], v.shape[0], 0, "", 0, 0)
            for a, v in enumerate(arrays[:5])
        ]
        quarter = w_latent.shape[1] // n_tensor
        plans.append((5, "zyxc", quarter, quarter, 0, "xc", quarter, 0))
        block, half_rows = rows_part // 2, n_expert * seq_len // 2
        plans += [
            (6, "zyxc", block, block, h * half_rows, "xc", rows_part, h * block) for h in range(2)
        ]
        small, query_full, keyval_full, outproj_full, routed_all, latent_t, dy_gathered = gather(
            arrays, plans, SIZES, 1
        )
        latent_t = latent_t.reshape(n_expert, -1, w_latent.shape[0])
        latent_t = jnp.swapaxes(latent_t, 0, 1).reshape(-1, D)
        routed_all = routed_all.reshape(n_expert * n_tensor, 2, block, experts_all)
        routed_all = jnp.swapaxes(routed_all, 0, 1).reshape(-1, experts_all)
        routed_all = jnp.pad(routed_all, ((0, 0), (0, 128 - experts_all)))
        shared_gate, shared_up, shared_down, query_full = lax.optimization_barrier(
            (shared_gate, shared_up, shared_down, query_full)
        )
        small = small.reshape(n_expert, rows * 128)
    else:
        small = lax.all_gather(small, "expert", axis=0)
        latent_t = lax.all_gather(w_latent, "expert", axis=0, tiled=True).T
        query_full = lax.all_gather(w_query, "expert", axis=0, tiled=True)
        keyval_full = lax.all_gather(w_keyval, "expert", axis=0, tiled=True)
        outproj_full = lax.all_gather(w_out, "expert", axis=0, tiled=True)
    gain_in_f = small[:, :n_gain].reshape(-1).astype(jnp.float32)
    gain_mid_f = small[:, n_gain : 2 * n_gain].reshape(-1).astype(jnp.float32)
    gain_lat_f = small[:, 2 * n_gain : 2 * n_gain + n_lat].reshape(-1).astype(jnp.float32)
    n_router = w_router.shape[0] * experts_all
    router_full = small[:, 2 * n_gain + n_lat :][:, :n_router].reshape(D, experts_all)
    heads_local = query_full.shape[1] // (NOPE + ROPE)

    sh_here = shared_gate.shape[1] // n_expert
    sh_rows = shared_gate.shape[0]
    units = expert_gate.shape[2]
    lengths = [units] * experts_here + [sh_here]
    shared_w = jnp.stack([shared_gate.T, shared_up.T, shared_down.T])
    shared_w = shared_w.reshape(3, n_expert, sh_here, sh_rows)
    if direct():
        segments_w = [-(-length // 128) * 128 for length in lengths]
        shared_w = jnp.pad(shared_w, ((0, 0), (0, 0), (0, -sh_here % 16), (0, 0)))
    else:
        segments_w = lengths
    shared_w = lax.all_to_all(shared_w, "expert", split_axis=1, concat_axis=0)
    starts = [sum(segments_w[:i]) for i in range(len(lengths))]
    gate_t, up_t = jnp.swapaxes(expert_gate, 1, 2), jnp.swapaxes(expert_up, 1, 2)
    if not direct():
        gate_t, up_t, down_w = [
            jnp.concatenate(
                [v[i] for i in range(experts_here)]
                + [jnp.swapaxes(shared_w[:, which], 0, 1).reshape(sh_here, D)]
            )
            for which, v in enumerate([gate_t, up_t, expert_down])
        ]

    tok_f = tokens.astype(jnp.float32)
    inv_in = inv_rms(tok_f)
    normed = (tok_f * inv_in * gain_in_f).astype(jnp.bfloat16)
    query_lin = dot_plain(normed, query_full).reshape(seq_len, heads_local, NOPE + ROPE)
    seg_ids = segments[0]
    cos_tab, sin_tab = rope_tables(doc_positions(seg_ids))
    q_nope = query_lin[..., :NOPE].astype(jnp.bfloat16)
    q_rope = rotate(query_lin[..., NOPE:], cos_tab[:, None, :], sin_tab[:, None, :]).astype(
        jnp.bfloat16
    )
    latent_all = dot_last(normed, latent_t)
    latent = latent_all[:, :KVR]
    inv_lat = inv_rms(latent)
    latent_n = (latent * inv_lat * gain_lat_f).astype(jnp.bfloat16)
    keyval = dot_plain(latent_n, keyval_full).reshape(seq_len, heads_local, NOPE + VD)
    key_nope = keyval[..., :NOPE].astype(jnp.bfloat16)
    values = keyval[..., NOPE:].astype(jnp.bfloat16)
    key_rope = rotate(latent_all[:, KVR:], cos_tab, sin_tab).astype(jnp.bfloat16)
    scores = masked_scores(q_nope, q_rope, key_nope, key_rope, seg_ids, seg_ids, 0)
    top_val = jnp.max(scores, axis=-1, keepdims=True)
    expo = jnp.exp(scores - top_val)
    probs = expo / jnp.sum(expo, axis=-1, keepdims=True)
    probs_b = probs.astype(jnp.bfloat16)
    attended = jnp.einsum("hqk,khd->qhd", probs_b, values, preferred_element_type=jnp.float32)
    attended = attended.astype(jnp.bfloat16).reshape(seq_len, heads_local * VD)
    attn_rows = scatter_tensor(dot_last(attended, outproj_full).astype(jnp.bfloat16), 2)

    residual = my_rows(tok_f) + attn_rows
    inv_mid = inv_rms(residual)
    normed_mid = (residual * inv_mid * gain_mid_f).astype(jnp.bfloat16)
    def routing(rows_in, mask):
        prob = jax.nn.sigmoid(dot_plain(rows_in, router_full))
        chosen = prob * mask
        chosen_sum = jnp.sum(chosen, axis=1, keepdims=True)
        return prob, chosen_sum, ROUTE_SCALE * chosen / chosen_sum

    routed_units = experts_here * units

    def mixture(normed_part, dy_part, route_part):
        normed_all = lax.all_gather(normed_part, both, axis=0, tiled=True)
        dy_all = lax.all_gather(dy_part, both, axis=0, tiled=True)
        mask_all = lax.all_gather(route_part, both, axis=0, tiled=True).astype(jnp.float32)
        n_all = normed_all.shape[0]
        weights_here = lax.dynamic_slice_in_dim(
            routing(normed_all, mask_all)[2], expert_pos * experts_here, experts_here, 1
        )
        scale = jnp.concatenate(
            [jnp.broadcast_to(weights_here[:, i : i + 1], (n_all, units)) for i in range(experts_here)]
            + [jnp.ones((n_all, sh_here), jnp.float32)],
            axis=1,
        )
        gate_x = dot_last(normed_all, gate_t)
        up_x = dot_last(normed_all, up_t)
        grad_h = dot_last(dy_all, down_w)
        sig_x = jax.nn.sigmoid(gate_x)
        silu_x = gate_x * sig_x
        hidden = silu_x * up_x
        hidden_s = (hidden * scale).astype(jnp.bfloat16)
        grad_gates = (grad_h * hidden)[:, :routed_units]
        grad_gates = jnp.sum(grad_gates.reshape(n_all, experts_here, units), axis=2)
        grad_hs = grad_h * scale
        grad_gate_x = (grad_hs * up_x * sig_x * (1.0 + gate_x * (1.0 - sig_x))).astype(jnp.bfloat16)
        grad_up_x = (grad_hs * silu_x).astype(jnp.bfloat16)
        out_x = dot_plain(hidden_s, down_w).astype(jnp.bfloat16)
        grad_x = (dot_plain(grad_gate_x, gate_t) + dot_plain(grad_up_x, up_t)).astype(jnp.bfloat16)
        grad_gates = lax.dynamic_update_slice_in_dim(
            jnp.zeros((n_all, experts_all), jnp.float32), grad_gates, expert_pos * experts_here, 1
        )
        grad_rows = lax.psum_scatter(grad_x, both, scatter_dimension=0, tiled=True)
        grad_gates = lax.psum_scatter(grad_gates, both, scatter_dimension=0, tiled=True)
        moe_rows = lax.psum_scatter(out_x, both, scatter_dimension=0, tiled=True)
        return (moe_rows, grad_rows, grad_gates), (
            dot_first(grad_gate_x, normed_all),
            dot_first(grad_up_x, normed_all),
            dot_first(hidden_s, dy_all),
        )

    inputs = (normed_mid, my_rows(cotangent), my_routed)
    pieces = max(1, n_expert * seq_len // 4096)
    if direct():
        router_w = jnp.pad(router_full, ((0, 0), (0, 128 - experts_all)))
        weights_w = (gate_t, up_t, expert_down, shared_w)
        x_all, hidden_s, grad_gate_up, gate_sums = mixture_forward(
            normed_mid, dy_gathered, routed_all, weights_w, router_w, segments_w, 3
        )
        sums, out_x, unit_rows = mixture_backward(
            hidden_s, grad_gate_up, gate_sums, residual, weights_w, segments_w, 5
        )
        sums, out_x = lax.optimization_barrier((sums, out_x))
        out_x = out_x.reshape(n_expert * n_tensor * seq_len, D // n_tensor)
        moe_rows = lax.psum_scatter(out_x, both, scatter_dimension=0, tiled=True)
        by_row = (moe_rows, sums[:, :D], sums[:, D : D + experts_all])
    elif pieces == 1:
        by_row, by_weight = mixture(*inputs)
    else:
        inputs = [v.reshape(pieces, rows_part // pieces, v.shape[1]) for v in inputs]
        total = tuple(jnp.zeros(gate_t.shape, jnp.float32) for _ in range(3))

        def one_piece(total, piece):
            rows_out, more = mixture(*piece)
            return tuple(a + b for a, b in zip(total, more)), rows_out

        by_weight, by_row = lax.scan(one_piece, total, inputs)
        by_row = tuple(v.reshape(rows_part, v.shape[2]) for v in by_row)
    moe_rows, grad_mid, grad_gates = by_row
    moe_rows, grad_mid = moe_rows.astype(jnp.float32), grad_mid.astype(jnp.float32)
    mask = my_routed.astype(jnp.float32)
    prob, chosen_sum, weights = routing(normed_mid, mask)
    grad_prob = (
        mask
        * (ROUTE_SCALE * grad_gates - jnp.sum(grad_gates * weights, axis=1, keepdims=True))
        / chosen_sum
    )
    grad_logit = grad_prob * prob * (1.0 - prob)
    grad_mid = grad_mid + jnp.dot(grad_logit, router_full.astype(jnp.float32).T, precision=HIGH)
    grad_router = jnp.dot(normed_mid.astype(jnp.float32).T, grad_logit, precision=HIGH)
    resid_part, grad_gain_mid = norm_back(residual, inv_mid, gain_mid_f, grad_mid)
    grad_resid = my_rows(cotangent).astype(jnp.float32) + resid_part
    grad_attn = gather_tensor(grad_resid.astype(jnp.bfloat16), 6)

    grad_outproj = dot_first(grad_attn, attended)
    grad_att = (
        dot_plain(grad_attn, outproj_full).astype(jnp.bfloat16).reshape(seq_len, heads_local, VD)
    )
    score_scale = (NOPE + ROPE) ** (-0.5)
    grad_probs = jnp.einsum("qhd,khd->hqk", grad_att, values, preferred_element_type=jnp.float32)
    delta_sum = jnp.sum(probs * grad_probs, axis=-1, keepdims=True)
    grad_scores = (probs * (grad_probs - delta_sum)).astype(jnp.bfloat16)
    grad_qn = (
        jnp.einsum("hqk,khd->qhd", grad_scores, key_nope, preferred_element_type=jnp.float32)
        * score_scale
    )
    grad_qr = (
        jnp.einsum("hqk,kd->qhd", grad_scores, key_rope, preferred_element_type=jnp.float32)
        * score_scale
    )
    grad_knope = (
        jnp.einsum("hqk,qhd->khd", grad_scores, q_nope, preferred_element_type=jnp.float32)
        * score_scale
    )
    grad_krope = (
        jnp.einsum("hqk,qhd->kd", grad_scores, q_rope, preferred_element_type=jnp.float32)
        * score_scale
    )
    grad_values = jnp.einsum(
        "hqk,qhd->khd", probs_b, grad_att, preferred_element_type=jnp.float32
    )
    grad_qr = unrotate(grad_qr, cos_tab[:, None, :], sin_tab[:, None, :])
    grad_query = (
        jnp.concatenate([grad_qn, grad_qr], axis=-1)
        .reshape(seq_len, heads_local * (NOPE + ROPE))
        .astype(jnp.bfloat16)
    )
    grad_wquery = dot_first(normed, grad_query)
    grad_normed = dot_last(grad_query, query_full)
    grad_keyval = (
        jnp.concatenate([grad_knope, grad_values], axis=-1)
        .reshape(seq_len, heads_local * (NOPE + VD))
        .astype(jnp.bfloat16)
    )
    grad_wkeyval = dot_first(latent_n, grad_keyval)
    grad_latent_n = dot_last(grad_keyval, keyval_full)
    grad_latent, grad_gain_lat = norm_back(latent, inv_lat, gain_lat_f, grad_latent_n)
    grad_latent_all = jnp.concatenate(
        [grad_latent, unrotate(grad_krope, cos_tab, sin_tab)], axis=-1
    )
    grad_latent_all = grad_latent_all.astype(jnp.bfloat16)
    grad_normed = grad_normed + dot_plain(grad_latent_all, latent_t)
    n_latent = w_latent.shape[1]
    if direct():
        grad_latent_all = jnp.pad(grad_latent_all, ((0, 0), (0, -n_latent % 128)))
    grad_wlatent = dot_first(normed, grad_latent_all)
    tok_part, grad_gain_in = norm_back(tok_f, inv_in, gain_in_f, grad_normed)

    n_dev = n_expert * n_tensor
    shared_small = [grad_gain_in, grad_gain_mid, grad_gain_lat, grad_router]
    shared_small = jnp.concatenate([v.reshape(n_dev, -1) for v in shared_small], axis=1)
    parts = [grad_wquery, grad_wkeyval, grad_outproj, grad_wlatent, shared_small, tok_part]
    parts = [v.astype(jnp.bfloat16) for v in parts]
    if direct():
        n_small = parts[4].shape[1]
        rows = -(-n_small // 2048) * 16
        parts[4] = jnp.pad(parts[4], ((0, 0), (0, rows * 128 - n_small))).reshape(-1, 128)
        orders = ["zy", "zy", "yz", "zyxc", "zyxc", "xc"]
        counts = [n_expert, n_expert, n_expert, n_dev, n_dev, n_tensor]
        plans = [
            (a, orders[a], v.shape[0] // counts[a], v.shape[0] // counts[a], 0)
            for a, v in enumerate(parts)
        ]
        a, order, rows, pitch, _ = plans[2]
        plans[2] = (a, order, rows // 2, pitch, 0)
        plans.append((a, order[::-1], rows // 2, pitch, rows // 2))
        (
            out_wquery, out_wkeyval, out_wout, out_wlatent, shared_small, tok_sum,
            out_egate, out_eup, out_edown, *shared_g,
        ) = final_sums(
            parts, plans, unit_rows, x_all, dy_gathered, segments_w, experts_here, units, sh_here, 7,
        )
        shared_small = shared_small.reshape(-1)[:n_small]
    else:
        axes = ["expert", "expert", "expert", both, both, "tensor"]
        out_wquery, out_wkeyval, out_wout, out_wlatent, shared_small, tok_sum = [
            lax.psum_scatter(v, axis, scatter_dimension=0, tiled=True).astype(jnp.float32)
            for v, axis in zip(parts, axes)
        ]
        shared_small = shared_small[0]
        out_egate, out_eup, out_edown = [
            jnp.stack([v[at : at + units] for at in starts[:-1]]) for v in by_weight
        ]
        shared_g = jnp.stack([v[starts[-1] : starts[-1] + sh_here] for v in by_weight])
        shared_g = shared_g.astype(jnp.bfloat16).reshape(3, sh_here, n_expert, sh_rows)
        shared_g = lax.all_to_all(shared_g, "expert", split_axis=2, concat_axis=1)
        shared_g = shared_g.reshape(3, n_expert * sh_here, sh_rows).astype(jnp.float32)
    out_egate, out_eup = jnp.swapaxes(out_egate, 1, 2), jnp.swapaxes(out_eup, 1, 2)
    tok_sum, moe_rows = lax.optimization_barrier((tok_sum, moe_rows))
    if direct():
        mixed = moe_rows.astype(jnp.bfloat16)
    else:
        mixed = (residual + moe_rows).astype(jnp.bfloat16)
        mixed = lax.all_to_all(
            mixed.reshape(rows_part, n_tensor, D // n_tensor), "tensor", split_axis=1, concat_axis=0
        ).reshape(seq_len, D // n_tensor)
    tokens_grad = (tok_sum + grad_resid).astype(jnp.bfloat16)
    n_gain, n_lat = D // n_dev, KVR // n_dev
    cuts = [n_gain, 2 * n_gain, 2 * n_gain + n_lat]
    out_gain_in, out_gain_mid, out_gain_lat, out_router = jnp.split(shared_small, cuts)
    return (
        mixed,
        tokens_grad,
        out_gain_in,
        out_wquery,
        out_wlatent[:, :n_latent],
        out_gain_lat,
        out_wkeyval,
        out_wout,
        out_gain_mid,
        out_router.reshape(D // n_dev, experts_all),
        shared_g[0].T,
        shared_g[1].T,
        shared_g[2].T,
        out_egate,
        out_eup,
        out_edown,
    )


def solution(mesh):
    in_specs = (
        P("expert", None),
        P("expert", None),
        P("expert", None),
        P("expert", None),
        P("expert"),
        P("expert", "tensor"),
        P("expert", None),
        P("expert"),
        P("expert", "tensor"),
        P("expert", "tensor"),
        P("expert"),
        P("expert", None),
        P("expert", "tensor"),
        P("expert", "tensor"),
        P("expert", "tensor"),
        P("expert", None, "tensor"),
        P("expert", None, "tensor"),
        P("expert", "tensor", None),
    )
    out_specs = (
        P("expert", "tensor"),
        P(("expert", "tensor"), None),
        P(("expert", "tensor")),
        P("expert", "tensor"),
        P(("expert", "tensor"), None),
        P(("expert", "tensor")),
        P("expert", "tensor"),
        P("expert", "tensor"),
        P(("expert", "tensor")),
        P(("expert", "tensor"), None),
        P("expert", "tensor"),
        P("expert", "tensor"),
        P("expert", "tensor"),
        P("expert", None, "tensor"),
        P("expert", None, "tensor"),
        P("expert", "tensor", None),
    )
    return jax.shard_map(local, mesh=mesh, in_specs=in_specs, out_specs=out_specs, check_vma=False)
```
